256 devices in a mesh: engine: 8 (over z_lo, core), ep: 32 (over y, z_hi, x).
Axes of the slice: x: 4, y: 4, z: 8 (z_hi: 2, z_lo: 4; z = z_hi * 4 + z_lo), core: 2. Of those that a mesh axis runs over, the one named last changes fastest.
Arguments:
- hidden_in: bfloat16 [65536, 7168], P(('engine', 'ep')), may hold values from -6 to 6
- expert_ids: int32 [65536, 8], P(('engine', 'ep')), may hold values from 0 to 255, all different within a row; in each aligned block of 256 rows (0 to 255, 256 to 511, ...) at most 16 rows name the same one
- route_weight: float32 [65536, 8], P(('engine', 'ep')), may hold values from 0.2 to 1
- gate_codes: bfloat16 [32, 7168, 256], P('ep', 'engine'), may hold values from -0.0625 to 0.0625
- gate_scales: bfloat16 [32, 56, 2], P('ep', 'engine'), may hold values from 0.29882812 to 3
- up_codes: bfloat16 [32, 7168, 256], P('ep', 'engine'), may hold values from -0.0625 to 0.0625
- up_scales: bfloat16 [32, 56, 2], P('ep', 'engine'), may hold values from 0.29882812 to 3
- down_codes: bfloat16 [32, 256, 7168], P('ep', None, 'engine'), may hold values from -0.125 to 0.125
- down_scales: bfloat16 [32, 2, 56], P('ep', None, 'engine'), may hold values from 0.29882812 to 3
- bucket_owner: int32 [32, 8], P('ep'), may hold values from 0 to 7, each once within a row
Outputs:
- mixed: bfloat16 [65536, 7168], P(('engine', 'ep'))
The draws below stay inside these ranges and needn't reach their ends.
Inputs may be any that keep to these rules, and one draw needn't show every extreme that they name: `expert_ids`: the 8 ids of one token differ; among the 256 tokens of one device no expert is named more than 16 times. `bucket_owner`: each row holds each engine index once.
All inputs are finite; a program needn't handle non-finite values.
Results may differ from the reference program's by a relative error of at most 0.0081.
Values may be sent and summed in bfloat16 or wider, within the bound.
A program may use at most 128 MiB of HBM per device.

```python
import math
import jax
import jax.numpy as jnp
import numpy as np
from jax import lax

D = 7168
EXPERTS_ALL = 256
TOP = 8
MOE_FF = 2048
SPLIT = 8
BLOCK = 128
TOK_DEV = 256
HID_DEV = 256
CAP = 16
TOKENS = 65536
N_ENGINE = 8
N_EP = 32


def shard_levels(key, shape, pieces, low, top_value):
    def one(axis_at, blocks):
        heights = jax.random.uniform(jax.random.fold_in(jax.random.fold_in(key, 6), axis_at), (blocks,), jnp.float32, low / len(pieces), top_value / len(pieces))
        return jnp.repeat(jnp.exp(heights), shape[axis_at] // blocks).reshape((-1,) + (1,) * (len(shape) - axis_at - 1))

    gain = one(*pieces[0])
    for cut in pieces[1:]:
        gain = gain * one(*cut)
    return gain


def deal_out(rng, own, number, rows, count, top, limit, slope):
    sequence = jax.random.permutation(rng, count)
    packed, common = portions_of(count, rows * top, limit, slope, True), portions_of(count, rows * top, limit, slope, False)
    places = jnp.arange(count)

    def named(sizes, rotation):
        used = int((sizes > 0).sum())
        fixed = max(1, used // 4)
        moved = fixed + (places - fixed + rotation * (used - fixed)) % max(1, count - fixed)
        return jnp.zeros((count,), jnp.int32).at[sequence[jnp.where(places < fixed, places, moved)]].set(jnp.asarray(sizes, jnp.int32))

    sizes = jnp.where(number % 4 == 0, named(packed, number // 4), named(common, number - number // 4 - 1))
    mixed = jax.random.permutation(jax.random.fold_in(own, 3), count)
    source_of, receiver = mixed[0:count // 2 * 2:2], mixed[1:count // 2 * 2:2]
    slack = jnp.minimum(sizes[source_of] - 1, limit - sizes[receiver]) // 2
    slack = jnp.where((source_of == sequence[0]) | (receiver == sequence[0]) | (sizes[receiver] == 0), 0, jnp.maximum(slack, 0))
    moved = jax.random.randint(jax.random.fold_in(own, 4), (count // 2,), 0, 1 << 20) % (slack + 1)
    sizes = sizes.at[source_of].add(-moved).at[receiver].add(moved)
    members = jnp.searchsorted(jnp.cumsum(sizes), jnp.arange(rows * top), side="right").astype(jnp.int32)
    listing = members.reshape(top, rows).T
    listing = listing[jax.random.permutation(jax.random.fold_in(own, 1), rows)]
    rotation = jax.random.randint(jax.random.fold_in(own, 2), (rows, 1), 0, top)
    return jnp.take_along_axis(listing, (jnp.arange(top)[None, :] + rotation) % top, axis=1)


def portions_of(number_of, total, most, skew, full):
    weights = [(1 << 20) // math.isqrt(standing ** skew) + 1 for standing in range(1, number_of + 1)]
    largest = most if full else min(most, max(-(-total // number_of), total * weights[0] // sum(weights)))
    least = 1 if total - largest >= number_of - 1 else 0
    counts, rest = [largest] + [least] * (number_of - 1), total - largest - least * (number_of - 1)
    while rest > 0:
        candidates = [i for i in range(1, number_of) if counts[i] < largest] or [i for i in range(1, number_of) if counts[i] < most]
        pool, remaining = sum([weights[i] for i in candidates]), rest
        for i in candidates:
            addition = min(most - counts[i], max(1, remaining * weights[i] // pool), rest)
            counts[i] = counts[i] + addition
            rest = rest - addition
    return np.array(counts)


def bell_draw(stream_key, dims, spread, most, cuts=(), kind=jnp.bfloat16):
    level = shard_levels(stream_key, dims, cuts, -0.22, 0.18) if cuts else 1.0
    entries = jax.random.normal(stream_key, dims, jnp.float32) * spread * level
    return jnp.minimum(jnp.maximum(entries, -most), most).astype(kind)


def setup_inputs(seed: int = 0) -> dict:
    key_of = jax.random.split(jax.random.key(seed), 11)
    hidden_in = bell_draw(key_of[0], (TOKENS, D), 1.0, 6.0, ((0, 256),))
    expert_ids_keys = jax.random.split(jax.random.fold_in(key_of[1], 1), TOKENS // TOK_DEV)
    expert_ids_turns = jax.random.permutation(jax.random.fold_in(key_of[1], 3), TOKENS // TOK_DEV)
    expert_ids = jax.vmap(lambda own, number: deal_out(jax.random.fold_in(key_of[1], 2), own, number, TOK_DEV, EXPERTS_ALL, TOP, CAP, 1))(expert_ids_keys, expert_ids_turns).reshape((TOKENS, TOP))
    route_weight = jnp.clip(0.2 + 0.8 * jax.random.uniform(key_of[2], (TOKENS, TOP), jnp.float32) ** shard_levels(key_of[2], (TOKENS, TOP), ((0, 256),), -0.2, 0.2), 0.2, 1.0)
    gate_codes = bell_draw(key_of[3], (N_EP, D, HID_DEV), D ** -0.5, 0.0625, ((0, 32), (1, 8)))
    gate_scales = jnp.clip(jnp.exp(math.log(3.0) - 2.306499 * jax.random.uniform(key_of[4], (N_EP, D // BLOCK, HID_DEV // BLOCK), jnp.float32) ** shard_levels(key_of[4], (N_EP, D // BLOCK, HID_DEV // BLOCK), ((0, 32), (1, 8)), -0.2, 0.2)), 0.29882812, 3.0).astype(jnp.bfloat16)
    up_codes = bell_draw(key_of[5], (N_EP, D, HID_DEV), D ** -0.5, 0.0625, ((0, 32), (1, 8)))
    up_scales = jnp.clip(jnp.exp(math.log(3.0) - 2.306499 * jax.random.uniform(key_of[6], (N_EP, D // BLOCK, HID_DEV // BLOCK), jnp.float32) ** shard_levels(key_of[6], (N_EP, D // BLOCK, HID_DEV // BLOCK), ((0, 32), (1, 8)), -0.2, 0.2)), 0.29882812, 3.0).astype(jnp.bfloat16)
    down_codes = bell_draw(key_of[7], (N_EP, HID_DEV, D), MOE_FF ** -0.5, 0.125, ((0, 32), (2, 8)))
    down_scales = jnp.clip(jnp.exp(math.log(3.0) - 2.306499 * jax.random.uniform(key_of[8], (N_EP, HID_DEV // BLOCK, D // BLOCK), jnp.float32) ** shard_levels(key_of[8], (N_EP, HID_DEV // BLOCK, D // BLOCK), ((0, 32), (2, 8)), -0.2, 0.2)), 0.29882812, 3.0).astype(jnp.bfloat16)
    bucket_owner = jax.vmap(lambda own: jax.random.permutation(own, N_ENGINE))(jax.random.split(key_of[9], N_EP)).reshape((N_EP, N_ENGINE)).astype(jnp.int32)
    return dict(hidden_in=hidden_in, expert_ids=expert_ids, route_weight=route_weight, gate_codes=gate_codes, gate_scales=gate_scales, up_codes=up_codes, up_scales=up_scales, down_codes=down_codes, down_scales=down_scales, bucket_owner=bucket_owner)


def dequantize(values, scale_blocks):
    row_count, col_count = values.shape
    blocks = values.astype(jnp.float32).reshape(row_count // BLOCK, BLOCK, col_count // BLOCK, BLOCK)
    scaled = blocks * scale_blocks.astype(jnp.float32)[:, None, :, None]
    return scaled.reshape(row_count, col_count).astype(jnp.bfloat16)


def order_rows(stored, owners):
    bucket_count = owners.shape[0]
    grouped = stored.reshape((bucket_count, stored.shape[0] // bucket_count) + stored.shape[1:])
    return jnp.take(grouped, owners, axis=0).reshape(stored.shape)


def order_columns(stored, owners):
    bucket_count = owners.shape[0]
    grouped = stored.reshape(stored.shape[0], bucket_count, stored.shape[1] // bucket_count)
    return jnp.take(grouped, owners, axis=1).reshape(stored.shape)


def routing_tables(choices, weights, experts, capacity):
    labels = jnp.arange(experts, dtype=jnp.int32)
    matches = (choices[:, :, None] == labels[None, None, :]).astype(jnp.int32)
    per_token = jnp.sum(matches, axis=1)
    before = jnp.cumsum(per_token, axis=0) - per_token
    slot_index = jnp.sum(matches * before[:, None, :], axis=2)
    is_live = jnp.sum(matches, axis=2)
    target = jnp.where(is_live > 0, choices * capacity + slot_index, -1).astype(jnp.int32)
    places = jnp.arange(experts * capacity, dtype=jnp.int32)
    matched = target[:, :, None] == places[None, None, :]
    placing = jnp.sum(matched.astype(jnp.float32), axis=1)
    combining = jnp.sum(jnp.where(matched, weights[:, :, None], jnp.float32(0.0)), axis=1)
    return placing, combining


def reference(hidden_in, expert_ids, route_weight, gate_codes, gate_scales, up_codes, up_scales, down_codes, down_scales, bucket_owner):
    experts = N_EP // SPLIT

    def expert_weights(index):
        owners = lax.dynamic_index_in_dim(bucket_owner, index, 0, keepdims=False)
        gate_w = dequantize(order_rows(gate_codes[index], owners), order_rows(gate_scales[index], owners))
        up_w = dequantize(order_rows(up_codes[index], owners), order_rows(up_scales[index], owners))
        down_w = dequantize(order_columns(down_codes[index], owners), order_columns(down_scales[index], owners))
        return gate_w, up_w, down_w

    gate_all, up_all, down_all = lax.map(expert_weights, jnp.arange(N_EP, dtype=jnp.int32))
    token_rows = hidden_in.reshape(N_ENGINE, N_EP, TOK_DEV, D)
    chosen = expert_ids.reshape(N_ENGINE, N_EP, TOK_DEV, TOP)
    weighting = route_weight.reshape(N_ENGINE, N_EP, TOK_DEV, TOP)

    def one_engine(inputs):
        engine_rows, engine_ids, engine_weights = inputs
        placing, combining = jax.vmap(lambda first, second: routing_tables(first, second, experts, CAP))(engine_ids, engine_weights)
        buffers = jnp.einsum("stp,std->spd", placing, engine_rows.astype(jnp.float32)).astype(jnp.bfloat16)
        grouped = buffers.reshape(N_EP, experts, CAP, D).transpose(1, 0, 2, 3).reshape(experts, N_EP * CAP, D)

        def one_expert(expert):
            expert_rows = lax.dynamic_index_in_dim(grouped, expert, 0, keepdims=False)
            total = jnp.zeros((N_EP * CAP, D), jnp.float32)
            for quarter in range(SPLIT):
                index = expert * SPLIT + quarter
                gate_w = lax.dynamic_index_in_dim(gate_all, index, 0, keepdims=False)
                up_w = lax.dynamic_index_in_dim(up_all, index, 0, keepdims=False)
                down_w = lax.dynamic_index_in_dim(down_all, index, 0, keepdims=False)
                gate_act = jnp.dot(expert_rows, gate_w, preferred_element_type=jnp.float32)
                up_act = jnp.dot(expert_rows, up_w, preferred_element_type=jnp.float32)
                hidden = (jax.nn.silu(gate_act) * up_act).astype(jnp.bfloat16)
                partial_out = jnp.dot(hidden, down_w, preferred_element_type=jnp.float32).astype(jnp.bfloat16)
                total = total + partial_out.astype(jnp.float32)
            return total.astype(jnp.bfloat16)

        outputs = lax.map(one_expert, jnp.arange(experts, dtype=jnp.int32))
        per_source = outputs.reshape(experts, N_EP, CAP, D).transpose(1, 0, 2, 3).reshape(N_EP, experts * CAP, D)
        mixed = jnp.einsum("stp,spd->std", combining, per_source.astype(jnp.float32), precision=lax.Precision.HIGHEST)
        return mixed.astype(jnp.bfloat16)

    mixed = lax.map(one_engine, (token_rows, chosen, weighting))
    return mixed.reshape(TOKENS, D)
```

```python
import functools

import jax
import jax.numpy as jnp
from jax import lax
from jax.experimental import pallas as pl
from jax.experimental.pallas import tpu as pltpu
from jax.sharding import PartitionSpec as P

D = 7168
BLOCK = 128
CAP = 16
NB = 8
BUCKET = D // NB
HID = 256
TOK = 256
LIVE = 4
SLOTS = LIVE * CAP
PLANE = 16
ROWS = PLANE * CAP
SUBS = (256, 256, 256, 128)
OFFS = (0, 256, 512, 768)
NJ = len(SUBS)
MESH = pl.DeviceIdType.MESH


def kernel(
    hid_hbm, ids_ref, rw_ref, gc_hbm, uc_hbm, dc_hbm, gs_ref, us_ref, ds_ref, own_ref,
    es_ref, comb_ref,
    G, U, Ds, X, S, hid_v, acc, H, Ps, Rs, row_tx, row_rx, row_sm, inv_sm, tab_sm,
    load_sem, hid_sem, ring_s, ring_r, dring_s, dring_r, sib_s, sib_r, dsib_s, dsib_r,
    disp_s, disp_r, ret_s, ret_r, row_s, row_r, row_l,
):
    eng = lax.axis_index("engine")
    ep = lax.axis_index("ep")
    z_lo, core = eng // 2, eng % 2
    x, z_hi, y = ep % 4, (ep // 4) % 2, ep // 8
    z = z_hi * 4 + z_lo
    me_xy = y * 4 + x

    def dev(xx, yy, zz, cc):
        return ((zz % 4) * 2 + cc, (yy * 2 + zz // 4) * 4 + xx)

    ring_dev = (dev(x, y, (z + 1) % 8, core), dev(x, y, (z + 7) % 8, core))
    sib_dev = dev(x, y, z, 1 - core)
    far_dev = dev(x, y, (z + 4) % 8, core)

    def plane_dev(d):
        xx, yy = (x + d % 4) % 4, (y + d // 4) % 4
        return xx, yy, dev(xx, yy, z, core)

    def slot_of(dz):
        return ((z + dz + 8) % 8) * 2 + core

    own = slot_of(0)

    loads = [
        pltpu.make_async_copy(gc_hbm.at[0], G.at[own], load_sem.at[0]),
        pltpu.make_async_copy(uc_hbm.at[0], U.at[own], load_sem.at[1]),
    ]
    for j in range(NJ):
        loads.append(
            pltpu.make_async_copy(
                dc_hbm.at[0, :, pl.ds(OFFS[j], SUBS[j])], Ds[j].at[own], load_sem.at[2 + j]
            )
        )
    for c in loads:
        c.start()
    hid_loads = [
        pltpu.make_async_copy(
            hid_hbm.at[:, pl.ds(b * BUCKET, BUCKET)], hid_v.at[b], hid_sem.at[b]
        )
        for b in range(NB)
    ]
    for c in hid_loads:
        c.start()

    barrier = pltpu.get_barrier_semaphore()
    for d in (ring_dev[0], ring_dev[1], sib_dev, far_dev):
        pl.semaphore_signal(barrier, inc=1, device_id=d, device_id_type=MESH)

    def greet(d, carry):
        pl.semaphore_signal(barrier, inc=1, device_id=plane_dev(d)[2], device_id_type=MESH)
        return carry

    lax.fori_loop(1, PLANE, greet, 0)

    lane = lax.broadcasted_iota(jnp.int32, (1, 256), 1)

    def scale_gu(buf, scale_ref):
        sc = scale_ref[0].astype(jnp.float32)
        wide = jnp.where(lane < BLOCK, sc[:, 0:1], sc[:, 1:2])
        for r in range(BUCKET // BLOCK):
            rows = pl.ds(r * BLOCK, BLOCK)
            buf[own, rows, :] = (
                buf[own, rows, :].astype(jnp.float32) * wide[r : r + 1, :]
            ).astype(jnp.bfloat16)

    def copy(src, dst, ssem, rsem, device):
        return pltpu.make_async_remote_copy(
            src_ref=src, dst_ref=dst, send_sem=ssem, recv_sem=rsem,
            device_id=device, device_id_type=MESH,
        )

    sends = []

    def start(c):
        c.start()
        sends.append(c)

    GU = (G, U)

    def gu_ring(w, hop, kind):
        s = slot_of(-hop if w == 0 else hop)
        return copy(
            GU[kind].at[s], GU[kind].at[s],
            ring_s.at[w, hop, kind], ring_r.at[w, hop, kind], ring_dev[w],
        )

    def gu_arrived(w, hop, kind):
        s = slot_of(-(hop + 1) if w == 0 else hop + 1)
        copy(
            GU[kind].at[s], GU[kind].at[s],
            ring_s.at[w, hop, kind], ring_r.at[w, hop, kind], ring_dev[w],
        ).wait_recv()

    def q_of(w, h):
        return 0 if h == 0 else (7 if h == 4 else (2 * h if w == 0 else 2 * h - 1))

    def gu_sib(w, h, kind):
        s = slot_of(-h if w == 0 else h)
        q = q_of(w, h)
        return copy(
            GU[kind].at[s], GU[kind].at[s], sib_s.at[q, kind], sib_r.at[q, kind], sib_dev
        )

    def gu_sib_arrived(w, h, kind):
        s = ((z + (-h if w == 0 else h) + 8) % 8) * 2 + 1 - core
        q = q_of(w, h)
        copy(
            GU[kind].at[s], GU[kind].at[s], sib_s.at[q, kind], sib_r.at[q, kind], sib_dev
        ).wait_recv()

    def d_part(j, s, w, far):
        if far:
            return Ds[j].at[s, pl.ds(w * 128, 128), :]
        return Ds[j].at[s]

    def d_ring(j, w, hop):
        s = slot_of(-hop if w == 0 else hop)
        ref = d_part(j, s, w, hop == 3)
        return copy(ref, ref, dring_s.at[j, w, hop], dring_r.at[j, w, hop], ring_dev[w])

    def d_arrived(j, w, hop):
        s = slot_of(-(hop + 1) if w == 0 else hop + 1)
        ref = d_part(j, s, w, hop == 3)
        copy(
            ref, ref, dring_s.at[j, w, hop], dring_r.at[j, w, hop], ring_dev[w]
        ).wait_recv()

    def d_sib(j, w, h):
        s = slot_of(-h if w == 0 else h)
        ref = d_part(j, s, w, h == 4)
        q = 8 if (h == 4 and w == 1) else q_of(w, h)
        return copy(ref, ref, dsib_s.at[j, q], dsib_r.at[j, q], sib_dev)

    def d_sib_arrived(j, w, h):
        s = ((z + (-h if w == 0 else h) + 8) % 8) * 2 + 1 - core
        ref = d_part(j, s, w, h == 4)
        q = 8 if (h == 4 and w == 1) else q_of(w, h)
        copy(ref, ref, dsib_s.at[j, q], dsib_r.at[j, q], sib_dev).wait_recv()

    loads[0].wait()
    scale_gu(G, gs_ref)
    pl.semaphore_wait(barrier, PLANE - 1 + 4)
    start(gu_ring(0, 0, 0))
    start(gu_ring(1, 0, 0))
    loads[1].wait()
    scale_gu(U, us_ref)
    start(gu_ring(0, 0, 1))
    start(gu_ring(1, 0, 1))
    start(gu_sib(0, 0, 0))
    start(gu_sib(0, 0, 1))

    owners = jnp.zeros((8, 128), jnp.int32)
    lane8 = lax.broadcasted_iota(jnp.int32, (8, 128), 1)
    for b in range(NB):
        owners = jnp.where(lane8 == b, own_ref[0, b], owners)
    row_tx[...] = owners
    row_copy = copy(row_tx, row_rx, row_s, row_r, far_dev)
    start(row_copy)

    expert_lane = (lane % SLOTS) // CAP
    slot_lane = (lane % CAP).astype(jnp.float32)
    picked = jnp.zeros((TOK, 256), jnp.float32)
    weight = jnp.zeros((TOK, 256), jnp.float32)
    for k in range(8):
        hit = ids_ref[:, k : k + 1] == expert_lane
        picked = jnp.where(hit, 1.0, picked)
        weight = jnp.where(hit, rw_ref[:, k : k + 1], weight)
    row_i = lax.broadcasted_iota(jnp.int32, (TOK, TOK), 0)
    col_i = lax.broadcasted_iota(jnp.int32, (TOK, TOK), 1)
    below = jnp.where(col_i < row_i, 1.0, 0.0).astype(jnp.bfloat16)
    before = jnp.dot(below, picked.astype(jnp.bfloat16), preferred_element_type=jnp.float32)
    place = jnp.where(before == slot_lane, picked, 0.0)
    combine = place * weight
    first = combine.astype(jnp.bfloat16)
    rest = combine - first.astype(jnp.float32)
    second = rest.astype(jnp.bfloat16)
    third = (rest - second.astype(jnp.float32)).astype(jnp.bfloat16)
    group = lane // SLOTS
    comb_ref[...] = jnp.where(
        group == 0,
        first.astype(jnp.float32),
        jnp.where(
            group == 1,
            second.astype(jnp.float32),
            jnp.where(group == 2, third.astype(jnp.float32), 0.0),
        ),
    ).astype(jnp.bfloat16)
    placing = place.T[:SLOTS, :].astype(jnp.bfloat16)

    for b in range(NB):
        hid_loads[b].wait()

    def gather(b, carry):
        S[b] = jnp.dot(placing, hid_v[b], preferred_element_type=jnp.float32).astype(
            jnp.bfloat16
        )
        return carry

    lax.fori_loop(0, NB, gather, 0)

    def rows16(i):
        return pl.ds(pl.multiple_of(i * CAP, CAP), CAP)

    def disp_copy(d, sx, sy):
        return copy(
            S.at[:, rows16(sy), :], X.at[:, rows16(me_xy), :],
            disp_s.at[d], disp_r.at[d], dev(sx, sy, z, core),
        )

    def disp_start(d, carry):
        xx, yy, _ = plane_dev(d)
        disp_copy(d, xx, yy).start()
        return carry

    lax.fori_loop(1, PLANE, disp_start, 0)
    X[:, rows16(me_xy), :] = S[:, rows16(y), :]

    dsc = ds_ref[0].astype(jnp.float32)
    for j in range(NJ):
        loads[2 + j].wait()
        for rb in range(HID // BLOCK):
            for k in range(SUBS[j] // BLOCK):
                cb = OFFS[j] // BLOCK + k
                at = (own, pl.ds(rb * BLOCK, BLOCK), pl.ds(k * BLOCK, BLOCK))
                Ds[j][at] = (
                    Ds[j][at].astype(jnp.float32) * dsc[rb : rb + 1, cb : cb + 1]
                ).astype(jnp.bfloat16)

    def d_own(j):
        start(d_ring(j, 0, 0))
        start(d_ring(j, 1, 0))
        start(d_sib(j, 0, 0))

    def gu_event(h, kind):
        for w in (0, 1):
            if h == 4 and kind != w:
                continue
            gu_arrived(w, h - 1, kind)
            if h < 3 or (h == 3 and kind == w):
                start(gu_ring(w, h, kind))
            start(gu_sib(w, h, kind))

    def d_event(j, h):
        for w in (0, 1):
            d_arrived(j, w, h - 1)
            if h < 4:
                start(d_ring(j, w, h))
            start(d_sib(j, w, h))

    gu_event(1, 0)

    row_copy.wait_recv()
    to_smem = pltpu.make_async_copy(row_rx, row_sm, row_l)
    to_smem.start()
    to_smem.wait()
    for b in range(NB):
        tab_sm[z_hi * NB + b] = own_ref[0, b]
        tab_sm[(1 - z_hi) * NB + b] = row_sm[0, b]
    for g in range(NB):
        mine, theirs = jnp.int32(0), jnp.int32(0)
        for b in range(1, NB):
            mine = jnp.where(own_ref[0, b] == g, b, mine)
            theirs = jnp.where(row_sm[0, b] == g, b, theirs)
        inv_sm[z_hi * NB + g] = mine
        inv_sm[(1 - z_hi) * NB + g] = theirs

    gu_event(1, 1)
    gu_event(2, 0)
    gu_event(2, 1)
    d_own(0)
    gu_event(3, 0)

    def disp_wait(d, carry):
        disp_copy(d, x, y).wait_recv()
        return carry

    lax.fori_loop(1, PLANE, disp_wait, 0)

    acc[...] = jnp.zeros_like(acc)

    def gu_block(r, carry):
        q = r // 2
        k = (q + 1) // 2
        zz = (z + k * (1 - 2 * ((q + 1) % 2)) + 8) % 8
        s = zz * 2 + (core + r) % 2
        p = zz // 4
        xb = X[inv_sm[s]]
        acc[p, 0] += jnp.dot(xb, G[s], preferred_element_type=jnp.float32)
        acc[p, 1] += jnp.dot(xb, U[s], preferred_element_type=jnp.float32)
        return carry

    for h in range(3):
        for w in (0, 1):
            if h == 0 and w == 1:
                continue
            gu_sib_arrived(w, h, 0)
            gu_sib_arrived(w, h, 1)
    lax.fori_loop(0, 10, gu_block, 0)

    gu_event(3, 1)
    d_event(0, 1)
    d_own(1)
    gu_event(4, 0)
    gu_event(4, 1)
    for w in (0, 1):
        gu_sib_arrived(w, 3, 0)
        gu_sib_arrived(w, 3, 1)
    lax.fori_loop(10, 14, gu_block, 0)
    d_event(0, 2)
    d_event(1, 1)
    gu_sib_arrived(0, 4, 0)
    gu_sib_arrived(1, 4, 1)
    lax.fori_loop(14, 16, gu_block, 0)
    for p in (0, 1):
        H[:, p * HID : (p + 1) * HID] = (jax.nn.silu(acc[p, 0]) * acc[p, 1]).astype(jnp.bfloat16)

    def ret_copy(j, d, xx, yy):
        return copy(
            Ps[j].at[:, rows16(yy * 4 + xx), :], Rs[j].at[:, rows16(x * 4 + y), :],
            ret_s.at[j, d], ret_r.at[j, d], dev(xx, yy, z, core),
        )

    def down(j):
        for h in range(5):
            for w in (0, 1):
                if h == 0 and w == 1:
                    continue
                d_sib_arrived(j, w, h)

        def one(b, carry):
            out = jnp.dot(
                H[:, :HID], Ds[j][tab_sm[b]], preferred_element_type=jnp.float32
            ) + jnp.dot(
                H[:, HID:], Ds[j][NB + tab_sm[NB + b]], preferred_element_type=jnp.float32
            )
            Ps[j][b] = out.astype(jnp.bfloat16)
            return carry

        lax.fori_loop(0, NB, one, 0)

        def send(d, carry):
            xx, yy, _ = plane_dev(d)
            ret_copy(j, d, xx, yy).start()
            return carry

        lax.fori_loop(1, PLANE, send, 0)
        Rs[j][:, rows16(x * 4 + y), :] = Ps[j][:, rows16(me_xy), :]

    def finish(j):
        def arrive(d, carry):
            ret_copy(j, d, x, y).wait_recv()
            return carry

        lax.fori_loop(1, PLANE, arrive, 0)
        for b in range(NB):
            total = Rs[j][b, 0:SLOTS, :].astype(jnp.float32)
            for xx in range(1, 4):
                total = total + Rs[j][b, xx * SLOTS : (xx + 1) * SLOTS, :].astype(jnp.float32)
            es_ref[:, b * BUCKET + OFFS[j] : b * BUCKET + OFFS[j] + SUBS[j]] = total.astype(
                jnp.bfloat16
            )

    d_event(0, 3)
    d_event(1, 2)
    d_own(2)
    d_event(0, 4)
    d_event(1, 3)
    down(0)
    d_event(2, 1)
    d_own(3)
    d_event(1, 4)
    d_event(2, 2)
    down(1)
    d_event(3, 1)
    d_event(2, 3)
    d_event(3, 2)
    d_event(2, 4)
    d_event(3, 3)
    down(2)
    d_event(3, 4)
    down(3)
    for j in range(NJ):
        finish(j)

    for c in sends:
        c.wait_send()

    def sent(d, carry):
        disp_copy(d, x, y).wait_send()
        for j in range(NJ):
            ret_copy(j, d, x, y).wait_send()
        return carry

    lax.fori_loop(1, PLANE, sent, 0)


def mix_kernel(comb_ref, es_ref, out_ref):
    es = es_ref[...]
    out_ref[...] = jnp.dot(
        comb_ref[...], jnp.concatenate([es, es, es, es], axis=0),
        preferred_element_type=jnp.float32,
    ).astype(jnp.bfloat16)


def on_device(
    hidden_in, expert_ids, route_weight, gate_codes, gate_scales, up_codes, up_scales,
    down_codes, down_scales, bucket_owner,
):
    vmem = pl.BlockSpec(memory_space=pltpu.VMEM)
    smem = pl.BlockSpec(memory_space=pltpu.SMEM)
    anys = pl.BlockSpec(memory_space=pl.ANY)
    dma = pltpu.SemaphoreType.DMA
    bf16 = jnp.bfloat16
    es, comb = pl.pallas_call(
        kernel,
        out_shape=(
            jax.ShapeDtypeStruct((SLOTS, D), bf16),
            jax.ShapeDtypeStruct((TOK, 256), bf16),
        ),
        in_specs=[anys, vmem, vmem, anys, anys, anys, vmem, vmem, vmem, smem],
        out_specs=(vmem, vmem),
        scratch_shapes=[
            pltpu.VMEM((16, BUCKET, HID), bf16),
            pltpu.VMEM((16, BUCKET, HID), bf16),
            [pltpu.VMEM((16, HID, s), bf16) for s in SUBS],
            pltpu.VMEM((NB, ROWS, BUCKET), bf16),
            pltpu.VMEM((NB, SLOTS, BUCKET), bf16),
            pltpu.VMEM((NB, TOK, BUCKET), bf16),
            pltpu.VMEM((2, 2, ROWS, HID), jnp.float32),
            pltpu.VMEM((ROWS, 2 * HID), bf16),
            [pltpu.VMEM((NB, ROWS, s), bf16) for s in SUBS],
            [pltpu.VMEM((NB, ROWS, s), bf16) for s in SUBS],
            pltpu.VMEM((8, 128), jnp.int32),
            pltpu.VMEM((8, 128), jnp.int32),
            pltpu.SMEM((8, 128), jnp.int32),
            pltpu.SMEM((16,), jnp.int32),
            pltpu.SMEM((16,), jnp.int32),
            dma((2 + NJ,)),
            dma((NB,)),
            dma((2, 4, 2)),
            dma((2, 4, 2)),
            dma((NJ, 2, 4)),
            dma((NJ, 2, 4)),
            dma((8, 2)),
            dma((8, 2)),
            dma((NJ, 9)),
            dma((NJ, 9)),
            dma((PLANE,)),
            dma((PLANE,)),
            dma((NJ, PLANE)),
            dma((NJ, PLANE)),
            dma(()),
            dma(()),
            dma(()),
        ],
        compiler_params=pltpu.CompilerParams(
            collective_id=0, has_side_effects=True, vmem_limit_bytes=56 * 1024 * 1024
        ),
        name="experts",
    )(
        hidden_in, expert_ids, route_weight, gate_codes, up_codes, down_codes,
        gate_scales, up_scales, down_scales, bucket_owner,
    )
    tile = 1024
    return pl.pallas_call(
        mix_kernel,
        grid=(D // tile,),
        out_shape=jax.ShapeDtypeStruct((TOK, D), bf16),
        in_specs=[
            pl.BlockSpec((TOK, 256), lambda i: (0, 0)),
            pl.BlockSpec((SLOTS, tile), lambda i: (0, i)),
        ],
        out_specs=pl.BlockSpec((TOK, tile), lambda i: (0, i)),
        name="mix",
    )(comb, es)


def solution(mesh):
    tokens = P(("engine", "ep"), None)
    in_specs = (
        tokens,
        tokens,
        tokens,
        P("ep", "engine", None),
        P("ep", "engine", None),
        P("ep", "engine", None),
        P("ep", "engine", None),
        P("ep", None, "engine"),
        P("ep", None, "engine"),
        P("ep", None),
    )
    return jax.shard_map(
        on_device, mesh=mesh, in_specs=in_specs, out_specs=tokens, check_vma=False
    )
```

```python
import jax
import jax.numpy as jnp
from jax import lax
from jax.experimental import pallas as pl
from jax.experimental.pallas import tpu as pltpu
from jax.sharding import PartitionSpec as P

D = 7168
BLOCK = 128
CAP = 16
NB = 8
BUCKET = D // NB
HALF = BUCKET // 2
HID = 256
TOK = 256
LIVE = 4
SLOTS = LIVE * CAP
PLANE = 16
ROWS = PLANE * CAP
SUB = 128
NJ = BUCKET // SUB
FROM = 3 * SLOTS
MESH = pl.DeviceIdType.MESH

SPREAD = (
    (1, 0), (0, 1), (3, 0), (0, 3), (1, 1), (3, 3), (2, 0), (0, 2),
    (1, 3), (3, 1), (2, 1), (1, 2), (2, 3), (3, 2), (2, 2),
)


def kernel(
    hid_hbm, ids_ref, rw_ref, gc_hbm, uc_hbm, dc_hbm, gs_ref, us_ref, ds_ref, own_ref,
    es_ref, comb_ref,
    G, U, Ds, X, S, hid_v, acc, H, Ps, As, Rs, row_tx, row_rx, row_sm, inv_sm, tab_sm,
    load_sem, hid_sem, gu_s, ring_r, d_s, dring_r, gsib_s, sib_r, dsib_s, dsib_r,
    disp_s, disp_r, ret_s, ret_ra, ret_r, row_s, row_r, row_l,
):
    eng = lax.axis_index("engine")
    ep = lax.axis_index("ep")
    z_lo, core = eng // 2, eng % 2
    x, z_hi, y = ep % 4, (ep // 4) % 2, ep // 8
    z = z_hi * 4 + z_lo
    me_xy = x * 4 + y
    x_right, x_left, x_far = (x + 1) % 4, (x + 3) % 4, (x + 2) % 4

    def dev(xx, yy, zz, cc):
        return ((zz % 4) * 2 + cc, (yy * 2 + zz // 4) * 4 + xx)

    ring_dev = (dev(x, y, (z + 1) % 8, core), dev(x, y, (z + 7) % 8, core))
    sib_dev = dev(x, y, z, 1 - core)
    far_dev = dev(x, y, (z + 4) % 8, core)

    def plane(xx, yy):
        return dev(xx, yy, z, core)

    def at(w, h, cc):
        return ((z + (8 - h if w == 0 else h)) % 8) * 2 + cc

    own = at(0, 0, core)

    loads = [
        pltpu.make_async_copy(gc_hbm.at[0], G.at[own], load_sem.at[0]),
        pltpu.make_async_copy(uc_hbm.at[0], U.at[own], load_sem.at[1]),
    ]
    for j in range(NJ):
        loads.append(
            pltpu.make_async_copy(
                dc_hbm.at[0, :, pl.ds(j * SUB, SUB)], Ds[j].at[own], load_sem.at[2 + j]
            )
        )
    for c in loads[:2]:
        c.start()

    barrier = pltpu.get_barrier_semaphore()
    greeted = [ring_dev[0], ring_dev[1], sib_dev, far_dev]
    greeted += [plane((x + dx) % 4, (y + dy) % 4) for dx, dy in SPREAD]
    for d in greeted:
        pl.semaphore_signal(barrier, inc=1, device_id=d, device_id_type=MESH)

    hid_loads = [
        pltpu.make_async_copy(
            hid_hbm.at[:, pl.ds(b * BUCKET, BUCKET)], hid_v.at[b], hid_sem.at[b]
        )
        for b in range(NB)
    ]
    for c in hid_loads + loads[2:]:
        c.start()

    def scale_gu(buf, scale_ref):
        sc = scale_ref[0].astype(jnp.float32)
        for r in range(BUCKET // BLOCK):
            for cb in range(HID // BLOCK):
                i = (own, pl.ds(r * BLOCK, BLOCK), pl.ds(cb * BLOCK, BLOCK))
                buf[i] = (
                    buf[i].astype(jnp.float32) * sc[cb : cb + 1, r : r + 1]
                ).astype(jnp.bfloat16)

    def copy(src, dst, ssem, rsem, device):
        return pltpu.make_async_remote_copy(
            src_ref=src, dst_ref=dst, send_sem=ssem, recv_sem=rsem,
            device_id=device, device_id_type=MESH,
        )

    GU = (G, U)

    def gu_part(kind, w, h, cc):
        s = at(w, h, cc)
        if h == 4:
            return GU[kind].at[s, pl.ds(w * HALF, HALF), :]
        return GU[kind].at[s]

    def gu_ring(kind, w, hop):
        s = at(w, hop, core)
        ref = GU[kind].at[s, pl.ds(w * HALF, HALF), :] if hop == 3 else GU[kind].at[s]
        return copy(ref, ref, gu_s.at[kind], ring_r.at[kind, w, hop], ring_dev[w])

    def gu_arrived(kind, w, h):
        ref = gu_part(kind, w, h, core)
        copy(ref, ref, gu_s.at[kind], ring_r.at[kind, w, h - 1], ring_dev[w]).wait_recv()

    def gu_sib(kind, w, h, cc):
        ref = gu_part(kind, w, h, cc)
        return copy(ref, ref, gsib_s.at[kind], sib_r.at[kind, w, h], sib_dev)

    def d_part(j, w, h, cc):
        s = at(w, h, cc)
        if h == 4:
            return Ds[j].at[s, pl.ds(w * BLOCK, BLOCK), :]
        return Ds[j].at[s]

    def d_ring(j, w, hop):
        s = at(w, hop, core)
        ref = Ds[j].at[s, pl.ds(w * BLOCK, BLOCK), :] if hop == 3 else Ds[j].at[s]
        return copy(ref, ref, d_s.at[j], dring_r.at[j, w, hop], ring_dev[w])

    def d_arrived(j, w, h):
        ref = d_part(j, w, h, core)
        copy(ref, ref, d_s.at[j], dring_r.at[j, w, h - 1], ring_dev[w]).wait_recv()

    def d_sib(j, w, h):
        ref = d_part(j, w, h, core)
        return copy(ref, ref, dsib_s.at[j], dsib_r.at[j], sib_dev)

    def gu_event(kind, h):
        for w in (0, 1):
            gu_arrived(kind, w, h)
            if h < 4:
                gu_ring(kind, w, h).start()
            gu_sib(kind, w, h, core).start()

    def gu_sib_wait(kind, h):
        for w in (0, 1):
            if h > 0 or w == 0:
                gu_sib(kind, w, h, 1 - core).wait_recv()

    def d_own(j):
        d_ring(j, 0, 0).start()
        d_ring(j, 1, 0).start()
        d_sib(j, 0, 0).start()

    def d_event(j, h):
        for w in (0, 1):
            d_arrived(j, w, h)
            if h < 4:
                d_ring(j, w, h).start()
            d_sib(j, w, h).start()

    loads[0].wait()
    scale_gu(G, gs_ref)
    pl.semaphore_wait(barrier, len(greeted))
    gu_ring(0, 0, 0).start()
    gu_ring(0, 1, 0).start()
    loads[1].wait()
    scale_gu(U, us_ref)
    gu_ring(1, 0, 0).start()
    gu_ring(1, 1, 0).start()
    gu_sib(0, 0, 0, core).start()
    gu_sib(1, 0, 0, core).start()

    slot = lax.broadcasted_iota(jnp.int32, (SLOTS, 1), 0)
    expert_of = slot // CAP
    place_of = (slot % CAP).astype(jnp.float32)
    picked = jnp.zeros((SLOTS, TOK), jnp.float32)
    weight = jnp.zeros((SLOTS, TOK), jnp.float32)
    for k in range(8):
        hit = ids_ref[k : k + 1, :] == expert_of
        picked = jnp.where(hit, 1.0, picked)
        weight = jnp.where(hit, rw_ref[k : k + 1, :], weight)
    row_i = lax.broadcasted_iota(jnp.int32, (TOK, TOK), 0)
    col_i = lax.broadcasted_iota(jnp.int32, (TOK, TOK), 1)
    earlier = jnp.where(row_i < col_i, 1.0, 0.0).astype(jnp.bfloat16)
    before = jnp.dot(picked.astype(jnp.bfloat16), earlier, preferred_element_type=jnp.float32)
    place = jnp.where(before == place_of, picked, 0.0)
    placing = place.astype(jnp.bfloat16)

    for b in range(NB):
        hid_loads[b].wait()
        S[b] = jnp.dot(placing, hid_v[b], preferred_element_type=jnp.float32).astype(
            jnp.bfloat16
        )

    def rows16(i):
        return pl.ds(pl.multiple_of(i * CAP, CAP), CAP)

    for dx, dy in SPREAD:
        xx, yy = (x + dx) % 4, (y + dy) % 4
        copy(
            S.at[:, rows16(yy), :], X.at[:, rows16(me_xy), :], disp_s, disp_r, plane(xx, yy)
        ).start()
    X[:, rows16(me_xy), :] = S[:, rows16(y), :]

    owners = jnp.zeros((8, 128), jnp.int32)
    lane8 = lax.broadcasted_iota(jnp.int32, (8, 128), 1)
    for b in range(NB):
        owners = jnp.where(lane8 == b, own_ref[0, b], owners)
    row_tx[...] = owners
    row_copy = copy(row_tx, row_rx, row_s, row_r, far_dev)
    row_copy.start()

    dsc = ds_ref[0].astype(jnp.float32)
    for j in range(NJ):
        loads[2 + j].wait()
        for rb in range(HID // BLOCK):
            i = (own, pl.ds(rb * BLOCK, BLOCK), slice(None))
            Ds[j][i] = (
                Ds[j][i].astype(jnp.float32) * dsc[rb : rb + 1, j : j + 1]
            ).astype(jnp.bfloat16)

    gu_event(0, 1)

    combine = place * weight
    first = combine.astype(jnp.bfloat16).astype(jnp.float32)
    second = (combine - first).astype(jnp.bfloat16).astype(jnp.float32)
    third = combine - first - second
    stacked = jnp.concatenate([first, second, third, jnp.zeros_like(third)], axis=0)
    comb_ref[...] = stacked.T.astype(jnp.bfloat16)

    row_copy.wait_recv()
    to_smem = pltpu.make_async_copy(row_rx, row_sm, row_l)
    to_smem.start()
    to_smem.wait()
    for b in range(NB):
        tab_sm[z_hi * NB + b] = own_ref[0, b]
        tab_sm[(1 - z_hi) * NB + b] = row_sm[0, b]
    for g in range(NB):
        mine, theirs = jnp.int32(0), jnp.int32(0)
        for b in range(1, NB):
            mine = jnp.where(own_ref[0, b] == g, b, mine)
            theirs = jnp.where(row_sm[0, b] == g, b, theirs)
        inv_sm[z_hi * NB + g] = mine
        inv_sm[(1 - z_hi) * NB + g] = theirs
    acc[...] = jnp.zeros_like(acc)

    def gu_block(r, carry):
        q = r // 2
        k = (q + 1) // 2
        zz = (z + k * (1 - 2 * ((q + 1) % 2)) + 8) % 8
        s = zz * 2 + (core + r) % 2
        p = zz // 4
        xb = X[inv_sm[s]]
        acc[p, 0] += jnp.dot(xb, G[s], preferred_element_type=jnp.float32)
        acc[p, 1] += jnp.dot(xb, U[s], preferred_element_type=jnp.float32)
        return carry

    def gu_blocks(lo, hi):
        lax.fori_loop(lo, hi, gu_block, 0)

    def rows(xx, yy):
        return rows16(xx * 4 + yy)

    def ret_copy(j, xx, yy, part):
        return copy(
            Ps[j].at[:, rows(xx, yy), :], Rs[j].at[:, rows(part, y), :],
            ret_s.at[j], ret_r.at[j], plane(xx, yy),
        )

    def down(j):
        copy(
            Ds[j].at[pl.ds(0, 8)], Ds[j].at[pl.ds(0, 8)], dsib_s.at[j], dsib_r.at[j], sib_dev
        ).wait_recv()
        for b in range(0, NB, 2):
            near = jnp.concatenate([Ds[j][tab_sm[b]], Ds[j][tab_sm[b + 1]]], axis=1)
            far = jnp.concatenate(
                [Ds[j][NB + tab_sm[NB + b]], Ds[j][NB + tab_sm[NB + b + 1]]], axis=1
            )
            out = jnp.dot(H[:, :HID], near, preferred_element_type=jnp.float32) + jnp.dot(
                H[:, HID:], far, preferred_element_type=jnp.float32
            )
            Ps[j][b] = out[:, :SUB].astype(jnp.bfloat16)
            Ps[j][b + 1] = out[:, SUB:].astype(jnp.bfloat16)
        for w, xx in ((0, x_right), (1, x_left)):
            some = pl.ds(pl.multiple_of(x_far * SLOTS + w * 32, 32), 32)
            copy(
                Ps[j].at[:, some, :], As[j].at[w], ret_s.at[j], ret_ra.at[j], plane(xx, y)
            ).start()
        for k in (0, 1):
            ret_copy(j, x_right, 2 + k, 1).start()
            ret_copy(j, x_left, k, 2).start()
        for dy in (1, 3, 2):
            ret_copy(j, x, (y + dy) % 4, 0).start()
        Rs[j][:, rows(0, y), :] = Ps[j][:, rows(x, y), :]

    def relay(j):
        copy(As[j], As[j], ret_s.at[j], ret_ra.at[j], sib_dev).wait_recv()
        for w, xx in ((0, x_right), (1, x_left)):
            some = pl.ds(pl.multiple_of(xx * SLOTS + w * 32, 32), 32)
            Ps[j][:, some, :] = (
                Ps[j][:, some, :].astype(jnp.float32) + As[j][w].astype(jnp.float32)
            ).astype(jnp.bfloat16)
        for k in (0, 1):
            ret_copy(j, x_right, k, 1).start()
            ret_copy(j, x_left, 2 + k, 2).start()

    def finish(j):
        got = Rs[j].at[:, pl.ds(0, 11 * CAP), :]
        copy(got, got, ret_s.at[j], ret_r.at[j], sib_dev).wait_recv()
        for b in range(NB):
            total = Rs[j][b, 0:SLOTS, :].astype(jnp.float32)
            for part in (1, 2):
                total = total + Rs[j][b, part * SLOTS : (part + 1) * SLOTS, :].astype(
                    jnp.float32
                )
            es_ref[:, b * BUCKET + j * SUB : b * BUCKET + (j + 1) * SUB] = total.astype(
                jnp.bfloat16
            )

    gu_event(1, 1)
    gu_event(0, 2)
    d_own(0)
    gu_event(1, 2)
    got = X.at[:, pl.ds(0, ROWS - CAP), :]
    copy(got, got, disp_s, disp_r, sib_dev).wait_recv()
    for h in (0, 1):
        for kind in (0, 1):
            gu_sib_wait(kind, h)
    gu_blocks(0, 6)
    d_event(0, 1)
    d_own(1)
    gu_event(0, 3)
    for kind in (0, 1):
        gu_sib_wait(kind, 2)
    gu_blocks(6, 10)
    d_event(0, 2)
    d_event(1, 1)
    gu_event(0, 4)
    gu_event(1, 3)
    for kind in (0, 1):
        gu_sib_wait(kind, 3)
    gu_blocks(10, 14)
    d_event(0, 3)
    d_event(1, 2)
    d_own(2)
    gu_event(1, 4)
    for kind in (0, 1):
        gu_sib_wait(kind, 4)
    gu_blocks(14, 16)
    for p in (0, 1):
        H[:, p * HID : (p + 1) * HID] = (jax.nn.silu(acc[p, 0]) * acc[p, 1]).astype(jnp.bfloat16)
    d_event(0, 4)
    d_event(1, 3)
    d_own(3)
    d_event(2, 1)
    down(0)
    d_event(3, 1)
    d_event(1, 4)
    d_event(2, 2)
    d_own(4)
    down(1)
    d_event(2, 3)
    relay(0)
    d_event(3, 2)
    d_event(4, 1)
    d_event(2, 4)
    relay(1)
    d_event(3, 3)
    d_own(5)
    down(2)
    finish(0)
    d_event(4, 2)
    d_event(5, 1)
    d_event(3, 4)
    relay(2)
    finish(1)
    d_event(4, 3)
    d_own(6)
    down(3)
    d_event(5, 2)
    relay(3)
    finish(2)
    d_event(6, 1)
    d_event(4, 4)
    down(4)
    d_event(5, 3)
    d_event(6, 2)
    d_event(5, 4)
    down(5)
    relay(4)
    finish(3)
    d_event(6, 3)
    d_event(6, 4)
    down(6)
    relay(5)
    finish(4)
    relay(6)
    finish(5)

    for kind in (0, 1):
        some = GU[kind].at[pl.ds(0, 7)]
        copy(some, some, gu_s.at[kind], ring_r.at[kind, 0, 0], sib_dev).wait_send()
        some = GU[kind].at[pl.ds(0, 8)]
        copy(some, some, gsib_s.at[kind], ring_r.at[kind, 0, 0], sib_dev).wait_send()
    copy(got, got, disp_s, disp_r, sib_dev).wait_send()
    row_copy.wait_send()
    for j in range(NJ):
        some = Ds[j].at[pl.ds(0, 7)]
        copy(some, some, d_s.at[j], dsib_r.at[j], sib_dev).wait_send()
        some = Ds[j].at[pl.ds(0, 8)]
        copy(some, some, dsib_s.at[j], dsib_r.at[j], sib_dev).wait_send()
    finish(6)
    for j in range(NJ):
        some = Ps[j].at[:, pl.ds(0, 2 * 32 + 11 * CAP), :]
        copy(some, some, ret_s.at[j], ret_r.at[j], sib_dev).wait_send()


TILES = 4
TILE = D // TILES


def mix_kernel(comb_hbm, es_hbm, out_hbm, comb_v, es_v, out_v, comb_sem, es_sem, out_sem):
    comb_load = pltpu.make_async_copy(comb_hbm, comb_v, comb_sem)
    comb_load.start()

    def cols(i):
        return pl.ds(i * TILE, TILE)

    es_loads = [
        pltpu.make_async_copy(es_hbm.at[:, cols(i)], es_v.at[:, cols(i)], es_sem.at[i])
        for i in range(TILES)
    ]
    for c in es_loads:
        c.start()
    comb_load.wait()
    stores = []
    for i in range(TILES):
        es_loads[i].wait()
        es = es_v[:, cols(i)]
        out_v[:, cols(i)] = jnp.dot(
            comb_v[...], jnp.concatenate([es, es, es, es], axis=0),
            preferred_element_type=jnp.float32,
        ).astype(jnp.bfloat16)
        stores.append(
            pltpu.make_async_copy(out_v.at[:, cols(i)], out_hbm.at[:, cols(i)], out_sem.at[i])
        )
        stores[-1].start()
    for c in stores:
        c.wait()


def on_device(
    hidden_in, expert_ids, route_weight, gate_codes, gate_scales, up_codes, up_scales,
    down_codes, down_scales, bucket_owner,
):
    vmem = pl.BlockSpec(memory_space=pltpu.VMEM)
    smem = pl.BlockSpec(memory_space=pltpu.SMEM)
    anys = pl.BlockSpec(memory_space=pl.ANY)
    dma = pltpu.SemaphoreType.DMA
    bf16 = jnp.bfloat16
    es, comb = pl.pallas_call(
        kernel,
        out_shape=(
            jax.ShapeDtypeStruct((SLOTS, D), bf16),
            jax.ShapeDtypeStruct((TOK, 256), bf16),
        ),
        in_specs=[anys, vmem, vmem, anys, anys, anys, vmem, vmem, vmem, smem],
        out_specs=(vmem, vmem),
        scratch_shapes=[
            pltpu.VMEM((16, BUCKET, HID), bf16),
            pltpu.VMEM((16, BUCKET, HID), bf16),
            [pltpu.VMEM((16, HID, SUB), bf16) for _ in range(NJ)],
            pltpu.VMEM((NB, ROWS, BUCKET), bf16),
            pltpu.VMEM((NB, SLOTS, BUCKET), bf16),
            pltpu.VMEM((NB, TOK, BUCKET), bf16),
            pltpu.VMEM((2, 2, ROWS, HID), jnp.float32),
            pltpu.VMEM((ROWS, 2 * HID), bf16),
            [pltpu.VMEM((NB, ROWS, SUB), bf16) for _ in range(NJ)],
            [pltpu.VMEM((2, NB, 32, SUB), bf16) for _ in range(NJ)],
            [pltpu.VMEM((NB, FROM, SUB), bf16) for _ in range(NJ)],
            pltpu.VMEM((8, 128), jnp.int32),
            pltpu.VMEM((8, 128), jnp.int32),
            pltpu.SMEM((8, 128), jnp.int32),
            pltpu.SMEM((16,), jnp.int32),
            pltpu.SMEM((16,), jnp.int32),
            dma((2 + NJ,)),
            dma((NB,)),
            dma((2,)),
            dma((2, 2, 4)),
            dma((NJ,)),
            dma((NJ, 2, 4)),
            dma((2,)),
            dma((2, 2, 5)),
            dma((NJ,)),
            dma((NJ,)),
            dma(()),
            dma(()),
            dma((NJ,)),
            dma((NJ,)),
            dma((NJ,)),
            dma(()),
            dma(()),
            dma(()),
        ],
        compiler_params=pltpu.CompilerParams(
            collective_id=0, has_side_effects=True, vmem_limit_bytes=56 * 1024 * 1024
        ),
        name="experts",
    )(
        hidden_in, expert_ids.T, route_weight.T, gate_codes, up_codes, down_codes,
        gate_scales.transpose(0, 2, 1), up_scales.transpose(0, 2, 1), down_scales, bucket_owner,
    )
    return pl.pallas_call(
        mix_kernel,
        out_shape=jax.ShapeDtypeStruct((TOK, D), bf16),
        in_specs=[anys, anys],
        out_specs=anys,
        scratch_shapes=[
            pltpu.VMEM((TOK, 256), bf16),
            pltpu.VMEM((SLOTS, D), bf16),
            pltpu.VMEM((TOK, D), bf16),
            dma(()),
            dma((TILES,)),
            dma((TILES,)),
        ],
        compiler_params=pltpu.CompilerParams(vmem_limit_bytes=56 * 1024 * 1024),
        name="mix",
    )(comb, es)


def solution(mesh):
    tokens = P(("engine", "ep"), None)
    in_specs = (
        tokens,
        tokens,
        tokens,
        P("ep", "engine", None),
        P("ep", "engine", None),
        P("ep", "engine", None),
        P("ep", "engine", None),
        P("ep", None, "engine"),
        P("ep", None, "engine"),
        P("ep", None),
    )
    return jax.shard_map(
        on_device, mesh=mesh, in_specs=in_specs, out_specs=tokens, check_vma=False
    )
```

```python
import jax
import jax.numpy as jnp
from jax import lax
from jax.experimental import pallas as pl
from jax.experimental.pallas import tpu as pltpu
from jax.sharding import PartitionSpec as P

D = 7168
BLOCK = 128
CAP = 16
NB = 8
BUCKET = D // NB
HALF = BUCKET // 2
HID = 256
TOK = 256
LIVE = 4
SLOTS = LIVE * CAP
PLANE = 16
ROWS = PLANE * CAP
SUB = 128
NJ = BUCKET // SUB
FROM = 3 * SLOTS
MESH = pl.DeviceIdType.MESH

SPREAD = (
    (1, 0), (0, 1), (3, 0), (0, 3), (1, 1), (3, 3), (2, 0), (0, 2),
    (1, 3), (3, 1), (2, 1), (1, 2), (2, 3), (3, 2), (2, 2),
)

PLAN = (
    "c0 b0 U1 a0",
    "b1 c1 a1 G1",
    "a2 U2 B0-2 B2-4",
    "B4-6 G2 B6-8 B8-10",
    "U3 G3 b2 c2",
    "a3 d0 B10-12 B12-14",
    "U4 G4 b3 e0",
    "B14-16 c3 a4 H",
    "d1 f0 Da b4",
    "e1 c4 Db d2",
    "g0 Dc Ra e2",
    "Rb d3 f1 Rc",
    "e3 g1 d4 f2",
    "Dd e4 Fa g2",
    "De f3 Fb Rd",
    "Fc g3 f4 Re",
    "Df g4 Fd Dg",
    "Fe Rf Rg Ff",
    "Fg",
)


def kernel(
    hid_hbm, ids_ref, rw_ref, gc_hbm, uc_hbm, dc_hbm, gs_ref, us_ref, ds_ref, own_ref,
    out_ref,
    comb, G, U, Ds, X, S, hid_v, acc, H, Ps, As, Rs, row_tx, row_rx, row_sm, inv_sm, tab_sm,
    load_sem, hid_sem, gu_s, ring_r, d_s, dring_r, gsib_s, sib_r, dsib_s, dsib_r,
    disp_s, disp_r, ret_s, ret_ra, ret_r, row_s, row_r, row_l,
):
    eng = lax.axis_index("engine")
    ep = lax.axis_index("ep")
    z_lo, core = eng // 2, eng % 2
    x, z_hi, y = ep % 4, (ep // 4) % 2, ep // 8
    z = z_hi * 4 + z_lo
    me_xy = x * 4 + y
    x_right, x_left, x_far = (x + 1) % 4, (x + 3) % 4, (x + 2) % 4

    def dev(xx, yy, zz, cc):
        return ((zz % 4) * 2 + cc, (yy * 2 + zz // 4) * 4 + xx)

    ring_dev = (dev(x, y, (z + 1) % 8, core), dev(x, y, (z + 7) % 8, core))
    sib_dev = dev(x, y, z, 1 - core)
    far_dev = dev(x, y, (z + 4) % 8, core)

    def plane(xx, yy):
        return dev(xx, yy, z, core)

    def at(w, h, cc):
        return ((z + (8 - h if w == 0 else h)) % 8) * 2 + cc

    own = at(0, 0, core)

    loads = [
        pltpu.make_async_copy(gc_hbm.at[0], G.at[own], load_sem.at[0]),
        pltpu.make_async_copy(uc_hbm.at[0], U.at[own], load_sem.at[1]),
    ]
    for j in range(NJ):
        loads.append(
            pltpu.make_async_copy(
                dc_hbm.at[0, :, pl.ds(j * SUB, SUB)], Ds[j].at[own], load_sem.at[2 + j]
            )
        )
    for c in loads[:2]:
        c.start()

    barrier = pltpu.get_barrier_semaphore()
    greeted = [ring_dev[0], ring_dev[1], sib_dev, far_dev]
    greeted += [plane((x + dx) % 4, (y + dy) % 4) for dx, dy in SPREAD]
    for d in greeted:
        pl.semaphore_signal(barrier, inc=1, device_id=d, device_id_type=MESH)

    hid_loads = [
        pltpu.make_async_copy(
            hid_hbm.at[:, pl.ds(b * BUCKET, BUCKET)], hid_v.at[b], hid_sem.at[b]
        )
        for b in range(NB)
    ]
    for c in hid_loads + loads[2:]:
        c.start()

    def scale_gu(buf, scale_ref):
        sc = scale_ref[0].astype(jnp.float32)
        for r in range(BUCKET // BLOCK):
            for cb in range(HID // BLOCK):
                i = (own, pl.ds(r * BLOCK, BLOCK), pl.ds(cb * BLOCK, BLOCK))
                buf[i] = (
                    buf[i].astype(jnp.float32) * sc[cb : cb + 1, r : r + 1]
                ).astype(jnp.bfloat16)

    def copy(src, dst, ssem, rsem, device):
        return pltpu.make_async_remote_copy(
            src_ref=src, dst_ref=dst, send_sem=ssem, recv_sem=rsem,
            device_id=device, device_id_type=MESH,
        )

    GU = (G, U)

    def gu_part(kind, w, h, cc):
        s = at(w, h, cc)
        if h == 4:
            return GU[kind].at[s, pl.ds(w * HALF, HALF), :]
        return GU[kind].at[s]

    def gu_ring(kind, w, hop):
        s = at(w, hop, core)
        ref = GU[kind].at[s, pl.ds(w * HALF, HALF), :] if hop == 3 else GU[kind].at[s]
        return copy(ref, ref, gu_s.at[kind], ring_r.at[kind, w, hop], ring_dev[w])

    def gu_arrived(kind, w, h):
        ref = gu_part(kind, w, h, core)
        copy(ref, ref, gu_s.at[kind], ring_r.at[kind, w, h - 1], ring_dev[w]).wait_recv()

    def gu_sib(kind, w, h, cc):
        ref = gu_part(kind, w, h, cc)
        return copy(ref, ref, gsib_s.at[kind], sib_r.at[kind, w, h], sib_dev)

    def d_part(j, w, h, cc):
        s = at(w, h, cc)
        if h == 4:
            return Ds[j].at[s, pl.ds(w * BLOCK, BLOCK), :]
        return Ds[j].at[s]

    def d_ring(j, w, hop):
        s = at(w, hop, core)
        ref = Ds[j].at[s, pl.ds(w * BLOCK, BLOCK), :] if hop == 3 else Ds[j].at[s]
        return copy(ref, ref, d_s.at[j], dring_r.at[j, w, hop], ring_dev[w])

    def d_arrived(j, w, h):
        ref = d_part(j, w, h, core)
        copy(ref, ref, d_s.at[j], dring_r.at[j, w, h - 1], ring_dev[w]).wait_recv()

    def d_sib(j, w, h):
        ref = d_part(j, w, h, core)
        return copy(ref, ref, dsib_s.at[j], dsib_r.at[j], sib_dev)

    def gu_event(kind, h):
        for w in (0, 1):
            gu_arrived(kind, w, h)
            if h < 4:
                gu_ring(kind, w, h).start()
        for w in (0, 1):
            gu_sib(kind, w, h, core).start()

    def gu_sib_wait(kind, h):
        for w in (0, 1):
            if h > 0 or w == 0:
                gu_sib(kind, w, h, 1 - core).wait_recv()

    def d_own(j):
        d_ring(j, 0, 0).start()
        d_ring(j, 1, 0).start()
        d_sib(j, 0, 0).start()

    def d_event(j, h):
        for w in (0, 1):
            d_arrived(j, w, h)
            if h < 4:
                d_ring(j, w, h).start()
        for w in (0, 1):
            d_sib(j, w, h).start()

    loads[0].wait()
    scale_gu(G, gs_ref)
    pl.semaphore_wait(barrier, len(greeted))
    gu_ring(0, 0, 0).start()
    gu_ring(0, 1, 0).start()
    loads[1].wait()
    scale_gu(U, us_ref)
    gu_ring(1, 0, 0).start()
    gu_ring(1, 1, 0).start()
    gu_sib(0, 0, 0, core).start()
    gu_sib(1, 0, 0, core).start()

    slot = lax.broadcasted_iota(jnp.int32, (SLOTS, 1), 0)
    expert_of = slot // CAP
    place_of = (slot % CAP).astype(jnp.float32)
    picked = jnp.zeros((SLOTS, TOK), jnp.float32)
    weight = jnp.zeros((SLOTS, TOK), jnp.float32)
    for k in range(8):
        hit = ids_ref[k : k + 1, :] == expert_of
        picked = jnp.where(hit, 1.0, picked)
        weight = jnp.where(hit, rw_ref[k : k + 1, :], weight)
    row_i = lax.broadcasted_iota(jnp.int32, (TOK, TOK), 0)
    col_i = lax.broadcasted_iota(jnp.int32, (TOK, TOK), 1)
    earlier = jnp.where(row_i < col_i, 1.0, 0.0).astype(jnp.bfloat16)
    before = jnp.dot(picked.astype(jnp.bfloat16), earlier, preferred_element_type=jnp.float32)
    place = jnp.where(before == place_of, picked, 0.0)
    placing = place.astype(jnp.bfloat16)

    for b in range(NB):
        hid_loads[b].wait()
        S[b] = jnp.dot(placing, hid_v[b], preferred_element_type=jnp.float32).astype(
            jnp.bfloat16
        )

    def rows16(i):
        return pl.ds(pl.multiple_of(i * CAP, CAP), CAP)

    for dx, dy in SPREAD:
        xx, yy = (x + dx) % 4, (y + dy) % 4
        copy(
            S.at[:, rows16(yy), :], X.at[:, rows16(me_xy), :], disp_s, disp_r, plane(xx, yy)
        ).start()
    X[:, rows16(me_xy), :] = S[:, rows16(y), :]

    owners = jnp.zeros((8, 128), jnp.int32)
    lane8 = lax.broadcasted_iota(jnp.int32, (8, 128), 1)
    for b in range(NB):
        owners = jnp.where(lane8 == b, own_ref[0, b], owners)
    row_tx[...] = owners
    row_copy = copy(row_tx, row_rx, row_s, row_r, far_dev)
    row_copy.start()

    dsc = ds_ref[0].astype(jnp.float32)
    for j in range(NJ):
        loads[2 + j].wait()
        for rb in range(HID // BLOCK):
            i = (own, pl.ds(rb * BLOCK, BLOCK), slice(None))
            Ds[j][i] = (
                Ds[j][i].astype(jnp.float32) * dsc[rb : rb + 1, j : j + 1]
            ).astype(jnp.bfloat16)

    combine = place * weight
    first = combine.astype(jnp.bfloat16).astype(jnp.float32)
    second = (combine - first).astype(jnp.bfloat16).astype(jnp.float32)
    third = combine - first - second
    stacked = jnp.concatenate([first, second, third, jnp.zeros_like(third)], axis=0)
    comb[...] = stacked.T.astype(jnp.bfloat16)

    row_copy.wait_recv()
    to_smem = pltpu.make_async_copy(row_rx, row_sm, row_l)
    to_smem.start()
    to_smem.wait()
    for b in range(NB):
        tab_sm[z_hi * NB + b] = own_ref[0, b]
        tab_sm[(1 - z_hi) * NB + b] = row_sm[0, b]
    for g in range(NB):
        mine, theirs = jnp.int32(0), jnp.int32(0)
        for b in range(1, NB):
            mine = jnp.where(own_ref[0, b] == g, b, mine)
            theirs = jnp.where(row_sm[0, b] == g, b, theirs)
        inv_sm[z_hi * NB + g] = mine
        inv_sm[(1 - z_hi) * NB + g] = theirs
    acc[...] = jnp.zeros_like(acc)

    def gu_block(r, carry):
        q = r // 2
        k = (q + 1) // 2
        zz = (z + k * (1 - 2 * ((q + 1) % 2)) + 8) % 8
        s = zz * 2 + (core + r) % 2
        p = zz // 4
        xb = X[inv_sm[s]]
        acc[p, 0] += jnp.dot(xb, G[s], preferred_element_type=jnp.float32)
        acc[p, 1] += jnp.dot(xb, U[s], preferred_element_type=jnp.float32)
        return carry

    def rows(xx, yy):
        return rows16(xx * 4 + yy)

    def ret_copy(j, xx, yy, part):
        return copy(
            Ps[j].at[:, rows(xx, yy), :], Rs[j].at[:, rows(part, y), :],
            ret_s.at[j], ret_r.at[j], plane(xx, yy),
        )

    def down(j):
        copy(
            Ds[j].at[pl.ds(0, 8)], Ds[j].at[pl.ds(0, 8)], dsib_s.at[j], dsib_r.at[j], sib_dev
        ).wait_recv()
        for b in range(0, NB, 2):
            near = jnp.concatenate([Ds[j][tab_sm[b]], Ds[j][tab_sm[b + 1]]], axis=1)
            far = jnp.concatenate(
                [Ds[j][NB + tab_sm[NB + b]], Ds[j][NB + tab_sm[NB + b + 1]]], axis=1
            )
            out = jnp.dot(H[:, :HID], near, preferred_element_type=jnp.float32) + jnp.dot(
                H[:, HID:], far, preferred_element_type=jnp.float32
            )
            Ps[j][b] = out[:, :SUB].astype(jnp.bfloat16)
            Ps[j][b + 1] = out[:, SUB:].astype(jnp.bfloat16)
        for w, xx in ((0, x_right), (1, x_left)):
            some = pl.ds(pl.multiple_of(x_far * SLOTS + w * 32, 32), 32)
            copy(
                Ps[j].at[:, some, :], As[j].at[w], ret_s.at[j], ret_ra.at[j], plane(xx, y)
            ).start()
        for k in (0, 1):
            ret_copy(j, x_right, 2 + k, 1).start()
            ret_copy(j, x_left, k, 2).start()
        for dy in (1, 3, 2):
            ret_copy(j, x, (y + dy) % 4, 0).start()
        Rs[j][:, rows(0, y), :] = Ps[j][:, rows(x, y), :]

    def relay(j):
        copy(As[j], As[j], ret_s.at[j], ret_ra.at[j], sib_dev).wait_recv()
        for w, xx in ((0, x_right), (1, x_left)):
            some = pl.ds(pl.multiple_of(xx * SLOTS + w * 32, 32), 32)
            Ps[j][:, some, :] = (
                Ps[j][:, some, :].astype(jnp.float32) + As[j][w].astype(jnp.float32)
            ).astype(jnp.bfloat16)
        for k in (0, 1):
            ret_copy(j, x_right, k, 1).start()
            ret_copy(j, x_left, 2 + k, 2).start()

    def finish(j):
        got = Rs[j].at[:, pl.ds(0, 11 * CAP), :]
        copy(got, got, ret_s.at[j], ret_r.at[j], sib_dev).wait_recv()
        sums = []
        for b in range(NB):
            total = Rs[j][b, 0:SLOTS, :].astype(jnp.float32)
            for part in (1, 2):
                total = total + Rs[j][b, part * SLOTS : (part + 1) * SLOTS, :].astype(
                    jnp.float32
                )
            sums.append(total.astype(jnp.bfloat16))
        for b in range(0, NB, 2):
            pair = jnp.concatenate(sums[b : b + 2], axis=1)
            mixed = jnp.dot(
                comb[...], jnp.concatenate([pair] * 4, axis=0),
                preferred_element_type=jnp.float32,
            ).astype(jnp.bfloat16)
            for k in (0, 1):
                at_col = (b + k) * BUCKET + j * SUB
                out_ref[:, at_col : at_col + SUB] = mixed[:, k * SUB : (k + 1) * SUB]

    got = X.at[:, pl.ds(0, ROWS - CAP), :]
    first_blocks = True
    for token in " ".join(PLAN).split():
        name, rest = token[0], token[1:]
        if name in "GU":
            kind, h = "GU".index(name), int(rest)
            gu_event(kind, h)
        elif name == "B":
            lo, hi = map(int, rest.split("-"))
            if first_blocks:
                first_blocks = False
                copy(got, got, disp_s, disp_r, sib_dev).wait_recv()
            if lo == 0 or lo % 4 == 2:
                for kind in (0, 1):
                    gu_sib_wait(kind, (lo + 2) // 4)
            lax.fori_loop(lo, hi, gu_block, 0)
        elif name == "H":
            for p in (0, 1):
                H[:, p * HID : (p + 1) * HID] = (
                    jax.nn.silu(acc[p, 0]) * acc[p, 1]
                ).astype(jnp.bfloat16)
        elif name == "D":
            down("abcdefg".index(rest))
        elif name == "R":
            relay("abcdefg".index(rest))
        elif name == "F":
            finish("abcdefg".index(rest))
        elif rest == "0":
            d_own("abcdefg".index(name))
        else:
            d_event("abcdefg".index(name), int(rest))

    for kind in (0, 1):
        some = GU[kind].at[pl.ds(0, 7)]
        copy(some, some, gu_s.at[kind], ring_r.at[kind, 0, 0], sib_dev).wait_send()
        some = GU[kind].at[pl.ds(0, 8)]
        copy(some, some, gsib_s.at[kind], ring_r.at[kind, 0, 0], sib_dev).wait_send()
    copy(got, got, disp_s, disp_r, sib_dev).wait_send()
    row_copy.wait_send()
    for j in range(NJ):
        some = Ds[j].at[pl.ds(0, 7)]
        copy(some, some, d_s.at[j], dsib_r.at[j], sib_dev).wait_send()
        some = Ds[j].at[pl.ds(0, 8)]
        copy(some, some, dsib_s.at[j], dsib_r.at[j], sib_dev).wait_send()
    for j in range(NJ):
        some = Ps[j].at[:, pl.ds(0, 2 * 32 + 11 * CAP), :]
        copy(some, some, ret_s.at[j], ret_r.at[j], sib_dev).wait_send()


def on_device(
    hidden_in, expert_ids, route_weight, gate_codes, gate_scales, up_codes, up_scales,
    down_codes, down_scales, bucket_owner,
):
    vmem = pl.BlockSpec(memory_space=pltpu.VMEM)
    smem = pl.BlockSpec(memory_space=pltpu.SMEM)
    anys = pl.BlockSpec(memory_space=pl.ANY)
    dma = pltpu.SemaphoreType.DMA
    bf16 = jnp.bfloat16
    return pl.pallas_call(
        kernel,
        out_shape=pltpu.VMEM((TOK, D), bf16),
        in_specs=[anys, vmem, vmem, anys, anys, anys, vmem, vmem, vmem, smem],
        out_specs=vmem,
        scratch_shapes=[
            pltpu.VMEM((TOK, 256), bf16),
            pltpu.VMEM((16, BUCKET, HID), bf16),
            pltpu.VMEM((16, BUCKET, HID), bf16),
            [pltpu.VMEM((16, HID, SUB), bf16) for _ in range(NJ)],
            pltpu.VMEM((NB, ROWS, BUCKET), bf16),
            pltpu.VMEM((NB, SLOTS, BUCKET), bf16),
            pltpu.VMEM((NB, TOK, BUCKET), bf16),
            pltpu.VMEM((2, 2, ROWS, HID), jnp.float32),
            pltpu.VMEM((ROWS, 2 * HID), bf16),
            [pltpu.VMEM((NB, ROWS, SUB), bf16) for _ in range(NJ)],
            [pltpu.VMEM((2, NB, 32, SUB), bf16) for _ in range(NJ)],
            [pltpu.VMEM((NB, FROM, SUB), bf16) for _ in range(NJ)],
            pltpu.VMEM((8, 128), jnp.int32),
            pltpu.VMEM((8, 128), jnp.int32),
            pltpu.SMEM((8, 128), jnp.int32),
            pltpu.SMEM((16,), jnp.int32),
            pltpu.SMEM((16,), jnp.int32),
            dma((2 + NJ,)),
            dma((NB,)),
            dma((2,)),
            dma((2, 2, 4)),
            dma((NJ,)),
            dma((NJ, 2, 4)),
            dma((2,)),
            dma((2, 2, 5)),
            dma((NJ,)),
            dma((NJ,)),
            dma(()),
            dma(()),
            dma((NJ,)),
            dma((NJ,)),
            dma((NJ,)),
            dma(()),
            dma(()),
            dma(()),
        ],
        compiler_params=pltpu.CompilerParams(
            collective_id=0, has_side_effects=True, vmem_limit_bytes=56 * 1024 * 1024
        ),
        name="experts",
    )(
        hidden_in, expert_ids.T, route_weight.T, gate_codes, up_codes, down_codes,
        gate_scales.transpose(0, 2, 1), up_scales.transpose(0, 2, 1), down_scales, bucket_owner,
    )


def solution(mesh):
    tokens = P(("engine", "ep"), None)
    in_specs = (
        tokens,
        tokens,
        tokens,
        P("ep", "engine", None),
        P("ep", "engine", None),
        P("ep", "engine", None),
        P("ep", "engine", None),
        P("ep", None, "engine"),
        P("ep", None, "engine"),
        P("ep", None),
    )
    return jax.shard_map(
        on_device, mesh=mesh, in_specs=in_specs, out_specs=tokens, check_vma=False
    )
```

```python
import jax
import jax.numpy as jnp
from jax import lax
from jax.experimental import pallas as pl
from jax.experimental.pallas import tpu as pltpu
from jax.sharding import PartitionSpec as P

D = 7168
BLOCK = 128
CAP = 16
NB = 8
BUCKET = D // NB
HALF = BUCKET // 2
HID = 256
TOK = 256
LIVE = 4
SLOTS = LIVE * CAP
PLANE = 16
ROWS = PLANE * CAP
SUB = 128
NJ = BUCKET // SUB
FROM = 3 * LIVE
MESH = pl.DeviceIdType.MESH

SPREAD = (
    (1, 0), (0, 1), (3, 0), (0, 3), (1, 1), (3, 3), (2, 0), (0, 2),
    (1, 3), (3, 1), (2, 1), (1, 2), (2, 3), (3, 2), (2, 2),
)

PLAN = (
    "a0 b0 G1 c0",
    "U1 a1 b1 G2",
    "c1 B0-2 U2 B2-4",
    "a2 B4-6 B6-8 B8-10",
    "G3 U3 b2 c2",
    "a3 d0 B10-12 B12-14",
    "G4 U4 b3 e0",
    "B14-16 c3 a4 H",
    "d1 f0 Da b4",
    "e1 c4 Db d2",
    "g0 Dc Ra e2",
    "Rb d3 f1 Rc",
    "e3 g1 d4 f2",
    "Dd e4 Fa g2",
    "De f3 Fb Rd",
    "Fc g3 f4 Re",
    "Df g4 Fd Dg",
    "Fe Rf Rg Ff",
    "Fg",
)


def kernel(
    hid_hbm, ids_ref, rw_ref, gc_hbm, uc_hbm, dc_hbm, gs_ref, us_ref, ds_ref, own_ref,
    out_ref,
    comb, G, U, Ds, X, S, hid_v, acc, H, Ps, As, Rs, row_tx, row_rx, row_sm, inv_sm, tab_sm,
    load_sem, hid_sem, gu_s, ring_r, d_s, dring_r, gsib_s, sib_r, dsib_s, dsib_r,
    disp_s, disp_r, ret_s, ret_ra, ret_r, row_s, row_r, row_l,
):
    eng = lax.axis_index("engine")
    ep = lax.axis_index("ep")
    z_lo, core = eng // 2, eng % 2
    x, z_hi, y = ep % 4, (ep // 4) % 2, ep // 8
    z = z_hi * 4 + z_lo
    me_xy = x * 4 + y
    x_right, x_left, x_far = (x + 1) % 4, (x + 3) % 4, (x + 2) % 4

    def dev(xx, yy, zz, cc):
        return ((zz % 4) * 2 + cc, (yy * 2 + zz // 4) * 4 + xx)

    ring_dev = (dev(x, y, (z + 1) % 8, core), dev(x, y, (z + 7) % 8, core))
    sib_dev = dev(x, y, z, 1 - core)
    far_dev = dev(x, y, (z + 4) % 8, core)

    def plane(xx, yy):
        return dev(xx, yy, z, core)

    def at(w, h, cc):
        return ((z + (8 - h if w == 0 else h)) % 8) * 2 + cc

    own = at(0, 0, core)

    loads = [
        pltpu.make_async_copy(gc_hbm.at[0], G.at[own], load_sem.at[0]),
        pltpu.make_async_copy(uc_hbm.at[0], U.at[own], load_sem.at[1]),
    ]
    for j in range(NJ):
        loads.append(
            pltpu.make_async_copy(
                dc_hbm.at[0, :, pl.ds(j * SUB, SUB)], Ds[j].at[own], load_sem.at[2 + j]
            )
        )
    for c in loads[:2]:
        c.start()

    barrier = pltpu.get_barrier_semaphore()
    greeted = [ring_dev[0], ring_dev[1], sib_dev, far_dev]
    greeted += [plane((x + dx) % 4, (y + dy) % 4) for dx, dy in SPREAD]
    for d in greeted:
        pl.semaphore_signal(barrier, inc=1, device_id=d, device_id_type=MESH)

    hid_loads = [
        pltpu.make_async_copy(
            hid_hbm.at[:, pl.ds(b * BUCKET, BUCKET)], hid_v.at[b], hid_sem.at[b]
        )
        for b in range(NB)
    ]
    for c in hid_loads + loads[2:]:
        c.start()

    def scale_gu(buf, scale_ref):
        sc = scale_ref[0].astype(jnp.float32)
        for r in range(BUCKET // BLOCK):
            for cb in range(HID // BLOCK):
                i = (own, pl.ds(r * BLOCK, BLOCK), pl.ds(cb * BLOCK, BLOCK))
                buf[i] = (
                    buf[i].astype(jnp.float32) * sc[cb : cb + 1, r : r + 1]
                ).astype(jnp.bfloat16)

    def copy(src, dst, ssem, rsem, device):
        return pltpu.make_async_remote_copy(
            src_ref=src, dst_ref=dst, send_sem=ssem, recv_sem=rsem,
            device_id=device, device_id_type=MESH,
        )

    GU = (G, U)

    def gu_part(kind, w, h, cc):
        s = at(w, h, cc)
        if h == 4:
            return GU[kind].at[s, pl.ds(w * HALF, HALF), :]
        return GU[kind].at[s]

    def gu_ring(kind, w, hop):
        s = at(w, hop, core)
        ref = GU[kind].at[s, pl.ds(w * HALF, HALF), :] if hop == 3 else GU[kind].at[s]
        return copy(ref, ref, gu_s.at[kind], ring_r.at[kind, w, hop], ring_dev[w])

    def gu_arrived(kind, w, h):
        ref = gu_part(kind, w, h, core)
        copy(ref, ref, gu_s.at[kind], ring_r.at[kind, w, h - 1], ring_dev[w]).wait_recv()

    def gu_sib(kind, w, h, cc):
        ref = gu_part(kind, w, h, cc)
        return copy(ref, ref, gsib_s.at[kind], sib_r.at[kind, w, h], sib_dev)

    def d_part(j, w, h, cc):
        s = at(w, h, cc)
        if h == 4:
            return Ds[j].at[s, pl.ds(w * BLOCK, BLOCK), :]
        return Ds[j].at[s]

    def d_ring(j, w, hop):
        s = at(w, hop, core)
        ref = Ds[j].at[s, pl.ds(w * BLOCK, BLOCK), :] if hop == 3 else Ds[j].at[s]
        return copy(ref, ref, d_s.at[j], dring_r.at[j, w, hop], ring_dev[w])

    def d_arrived(j, w, h):
        ref = d_part(j, w, h, core)
        copy(ref, ref, d_s.at[j], dring_r.at[j, w, h - 1], ring_dev[w]).wait_recv()

    def d_sib(j, w, h):
        ref = d_part(j, w, h, core)
        return copy(ref, ref, dsib_s.at[j], dsib_r.at[j], sib_dev)

    def gu_event(kind, h):
        for w in (0, 1):
            gu_arrived(kind, w, h)
            if h < 4:
                gu_ring(kind, w, h).start()
        for w in (0, 1):
            gu_sib(kind, w, h, core).start()

    def gu_sib_wait(kind, h):
        for w in (0, 1):
            if h > 0 or w == 0:
                gu_sib(kind, w, h, 1 - core).wait_recv()

    def d_own(j):
        d_ring(j, 0, 0).start()
        d_ring(j, 1, 0).start()
        d_sib(j, 0, 0).start()

    def d_event(j, h):
        for w in (0, 1):
            d_arrived(j, w, h)
            if h < 4:
                d_ring(j, w, h).start()
            else:
                d_sib(j, w, h).start()
        for w in (0, 1) if h < 4 else ():
            d_sib(j, w, h).start()

    loads[0].wait()
    scale_gu(G, gs_ref)
    pl.semaphore_wait(barrier, len(greeted))
    gu_ring(0, 0, 0).start()
    gu_ring(0, 1, 0).start()
    loads[1].wait()
    scale_gu(U, us_ref)
    gu_ring(1, 0, 0).start()
    gu_ring(1, 1, 0).start()
    gu_sib(0, 0, 0, core).start()
    gu_sib(1, 0, 0, core).start()

    slot = lax.broadcasted_iota(jnp.int32, (SLOTS, 1), 0)
    expert_of = slot // CAP
    place_of = (slot % CAP).astype(jnp.float32)
    picked = jnp.zeros((SLOTS, TOK), jnp.float32)
    weight = jnp.zeros((SLOTS, TOK), jnp.float32)
    for k in range(8):
        hit = ids_ref[k : k + 1, :] == expert_of
        picked = jnp.where(hit, 1.0, picked)
        weight = jnp.where(hit, rw_ref[k : k + 1, :], weight)
    row_i = lax.broadcasted_iota(jnp.int32, (TOK, TOK), 0)
    col_i = lax.broadcasted_iota(jnp.int32, (TOK, TOK), 1)
    earlier = jnp.where(row_i < col_i, 1.0, 0.0).astype(jnp.bfloat16)
    before = jnp.dot(picked.astype(jnp.bfloat16), earlier, preferred_element_type=jnp.float32)
    place = jnp.where(before == place_of, picked, 0.0)
    placing = place.astype(jnp.bfloat16)

    for b in range(NB):
        hid_loads[b].wait()
        S[b] = jnp.dot(placing, hid_v[b], preferred_element_type=jnp.float32).astype(
            jnp.bfloat16
        )

    def rows16(i):
        return pl.ds(pl.multiple_of(i * CAP, CAP), CAP)

    for dx, dy in SPREAD:
        xx, yy = (x + dx) % 4, (y + dy) % 4
        copy(
            S.at[:, rows16(yy), :], X.at[:, rows16(me_xy), :], disp_s, disp_r, plane(xx, yy)
        ).start()
    X[:, rows16(me_xy), :] = S[:, rows16(y), :]

    owners = jnp.zeros((8, 128), jnp.int32)
    lane8 = lax.broadcasted_iota(jnp.int32, (8, 128), 1)
    for b in range(NB):
        owners = jnp.where(lane8 == b, own_ref[0, b], owners)
    row_tx[...] = owners
    row_copy = copy(row_tx, row_rx, row_s, row_r, far_dev)
    row_copy.start()

    dsc = ds_ref[0].astype(jnp.float32)
    for j in range(NJ):
        loads[2 + j].wait()
        for rb in range(HID // BLOCK):
            i = (own, pl.ds(rb * BLOCK, BLOCK), slice(None))
            Ds[j][i] = (
                Ds[j][i].astype(jnp.float32) * dsc[rb : rb + 1, j : j + 1]
            ).astype(jnp.bfloat16)

    combine = place * weight
    first = combine.astype(jnp.bfloat16).astype(jnp.float32)
    second = (combine - first).astype(jnp.bfloat16).astype(jnp.float32)
    third = combine - first - second
    stacked = jnp.concatenate([first, second, third, jnp.zeros_like(third)], axis=0)
    comb[...] = stacked.T.astype(jnp.bfloat16)

    row_copy.wait_recv()
    to_smem = pltpu.make_async_copy(row_rx, row_sm, row_l)
    to_smem.start()
    to_smem.wait()
    for b in range(NB):
        tab_sm[z_hi * NB + b] = own_ref[0, b]
        tab_sm[(1 - z_hi) * NB + b] = row_sm[0, b]
    for g in range(NB):
        mine, theirs = jnp.int32(0), jnp.int32(0)
        for b in range(1, NB):
            mine = jnp.where(own_ref[0, b] == g, b, mine)
            theirs = jnp.where(row_sm[0, b] == g, b, theirs)
        inv_sm[z_hi * NB + g] = mine
        inv_sm[(1 - z_hi) * NB + g] = theirs
    acc[...] = jnp.zeros_like(acc)

    def gu_block(r, carry):
        q = r // 2
        k = (q + 1) // 2
        zz = (z + k * (1 - 2 * ((q + 1) % 2)) + 8) % 8
        s = zz * 2 + (core + r) % 2
        p = zz // 4
        xb = X[inv_sm[s]]
        acc[p, 0] += jnp.dot(xb, G[s], preferred_element_type=jnp.float32)
        acc[p, 1] += jnp.dot(xb, U[s], preferred_element_type=jnp.float32)
        return carry

    def ret_copy(j, xx, yy, part):
        return copy(
            Ps[j].at[xx * 4 + yy], Rs[j].at[part * 4 + y],
            ret_s.at[j], ret_r.at[j], plane(xx, yy),
        )

    def down(j):
        copy(
            Ds[j].at[pl.ds(0, 8)], Ds[j].at[pl.ds(0, 8)], dsib_s.at[j], dsib_r.at[j], sib_dev
        ).wait_recv()
        for b in range(0, NB, 2):
            near = jnp.concatenate([Ds[j][tab_sm[b]], Ds[j][tab_sm[b + 1]]], axis=1)
            far = jnp.concatenate(
                [Ds[j][NB + tab_sm[NB + b]], Ds[j][NB + tab_sm[NB + b + 1]]], axis=1
            )
            out = jnp.dot(H[:, :HID], near, preferred_element_type=jnp.float32) + jnp.dot(
                H[:, HID:], far, preferred_element_type=jnp.float32
            )
            out = out.astype(jnp.bfloat16)
            Ps[j][:, b] = out[:, :SUB].reshape(PLANE, CAP, SUB)
            Ps[j][:, b + 1] = out[:, SUB:].reshape(PLANE, CAP, SUB)
        for w, xx in ((0, x_right), (1, x_left)):
            some = Ps[j].at[pl.ds(x_far * 4 + w * 2, 2)]
            copy(some, As[j].at[w], ret_s.at[j], ret_ra.at[j], plane(xx, y)).start()
        for k in (0, 1):
            ret_copy(j, x_right, 2 + k, 1).start()
            ret_copy(j, x_left, k, 2).start()
        for dy in (1, 3, 2):
            ret_copy(j, x, (y + dy) % 4, 0).start()
        Rs[j][y] = Ps[j][x * 4 + y]

    def relay(j):
        copy(As[j], As[j], ret_s.at[j], ret_ra.at[j], sib_dev).wait_recv()
        for w, xx in ((0, x_right), (1, x_left)):
            some = pl.ds(xx * 4 + w * 2, 2)
            Ps[j][some] = (
                Ps[j][some].astype(jnp.float32) + As[j][w].astype(jnp.float32)
            ).astype(jnp.bfloat16)
        for k in (0, 1):
            ret_copy(j, x_right, k, 1).start()
            ret_copy(j, x_left, 2 + k, 2).start()

    def finish(j):
        some = Rs[j].at[pl.ds(0, 11)]
        copy(some, some, ret_s.at[j], ret_r.at[j], sib_dev).wait_recv()
        sums = []
        for b in range(NB):
            total = Rs[j][0:4, b].astype(jnp.float32)
            for part in (1, 2):
                total = total + Rs[j][part * 4 : part * 4 + 4, b].astype(jnp.float32)
            sums.append(total.astype(jnp.bfloat16).reshape(SLOTS, SUB))
        for b in range(0, NB, 2):
            pair = jnp.concatenate(sums[b : b + 2], axis=1)
            mixed = jnp.dot(
                comb[...], jnp.concatenate([pair] * 4, axis=0),
                preferred_element_type=jnp.float32,
            ).astype(jnp.bfloat16)
            for k in (0, 1):
                at_col = (b + k) * BUCKET + j * SUB
                out_ref[:, at_col : at_col + SUB] = mixed[:, k * SUB : (k + 1) * SUB]

    got = X.at[:, pl.ds(0, ROWS - CAP), :]
    first_blocks = True
    for token in " ".join(PLAN).split():
        name, rest = token[0], token[1:]
        if name in "GU":
            kind, h = "GU".index(name), int(rest)
            gu_event(kind, h)
        elif name == "B":
            lo, hi = map(int, rest.split("-"))
            if first_blocks:
                first_blocks = False
                copy(got, got, disp_s, disp_r, sib_dev).wait_recv()
            if lo == 0 or lo % 4 == 2:
                for kind in (0, 1):
                    gu_sib_wait(kind, (lo + 2) // 4)
            lax.fori_loop(lo, hi, gu_block, 0)
        elif name == "H":
            for p in (0, 1):
                H[:, p * HID : (p + 1) * HID] = (
                    jax.nn.silu(acc[p, 0]) * acc[p, 1]
                ).astype(jnp.bfloat16)
        elif name == "D":
            down("abcdefg".index(rest))
        elif name == "R":
            relay("abcdefg".index(rest))
        elif name == "F":
            finish("abcdefg".index(rest))
        elif rest == "0":
            d_own("abcdefg".index(name))
        else:
            d_event("abcdefg".index(name), int(rest))

    for kind in (0, 1):
        some = GU[kind].at[pl.ds(0, 7)]
        copy(some, some, gu_s.at[kind], ring_r.at[kind, 0, 0], sib_dev).wait_send()
        some = GU[kind].at[pl.ds(0, 8)]
        copy(some, some, gsib_s.at[kind], ring_r.at[kind, 0, 0], sib_dev).wait_send()
    copy(got, got, disp_s, disp_r, sib_dev).wait_send()
    row_copy.wait_send()
    for j in range(NJ):
        some = Ds[j].at[pl.ds(0, 7)]
        copy(some, some, d_s.at[j], dsib_r.at[j], sib_dev).wait_send()
        some = Ds[j].at[pl.ds(0, 8)]
        copy(some, some, dsib_s.at[j], dsib_r.at[j], sib_dev).wait_send()
    for j in range(NJ):
        some = Ps[j].at[pl.ds(0, 15)]
        copy(some, some, ret_s.at[j], ret_r.at[j], sib_dev).wait_send()


def on_device(
    hidden_in, expert_ids, route_weight, gate_codes, gate_scales, up_codes, up_scales,
    down_codes, down_scales, bucket_owner,
):
    vmem = pl.BlockSpec(memory_space=pltpu.VMEM)
    smem = pl.BlockSpec(memory_space=pltpu.SMEM)
    anys = pl.BlockSpec(memory_space=pl.ANY)
    dma = pltpu.SemaphoreType.DMA
    bf16 = jnp.bfloat16
    return pl.pallas_call(
        kernel,
        out_shape=pltpu.VMEM((TOK, D), bf16),
        in_specs=[anys, vmem, vmem, anys, anys, anys, vmem, vmem, vmem, smem],
        out_specs=vmem,
        scratch_shapes=[
            pltpu.VMEM((TOK, 256), bf16),
            pltpu.VMEM((16, BUCKET, HID), bf16),
            pltpu.VMEM((16, BUCKET, HID), bf16),
            [pltpu.VMEM((16, HID, SUB), bf16) for _ in range(NJ)],
            pltpu.VMEM((NB, ROWS, BUCKET), bf16),
            pltpu.VMEM((NB, SLOTS, BUCKET), bf16),
            pltpu.VMEM((NB, TOK, BUCKET), bf16),
            pltpu.VMEM((2, 2, ROWS, HID), jnp.float32),
            pltpu.VMEM((ROWS, 2 * HID), bf16),
            [pltpu.VMEM((PLANE, NB, CAP, SUB), bf16) for _ in range(NJ)],
            [pltpu.VMEM((2, 2, NB, CAP, SUB), bf16) for _ in range(NJ)],
            [pltpu.VMEM((FROM, NB, CAP, SUB), bf16) for _ in range(NJ)],
            pltpu.VMEM((8, 128), jnp.int32),
            pltpu.VMEM((8, 128), jnp.int32),
            pltpu.SMEM((8, 128), jnp.int32),
            pltpu.SMEM((16,), jnp.int32),
            pltpu.SMEM((16,), jnp.int32),
            dma((2 + NJ,)),
            dma((NB,)),
            dma((2,)),
            dma((2, 2, 4)),
            dma((NJ,)),
            dma((NJ, 2, 4)),
            dma((2,)),
            dma((2, 2, 5)),
            dma((NJ,)),
            dma((NJ,)),
            dma(()),
            dma(()),
            dma((NJ,)),
            dma((NJ,)),
            dma((NJ,)),
            dma(()),
            dma(()),
            dma(()),
        ],
        compiler_params=pltpu.CompilerParams(
            collective_id=0, has_side_effects=True, vmem_limit_bytes=56 * 1024 * 1024
        ),
        name="experts",
    )(
        hidden_in, expert_ids.T, route_weight.T, gate_codes, up_codes, down_codes,
        gate_scales.transpose(0, 2, 1), up_scales.transpose(0, 2, 1), down_scales, bucket_owner,
    )


def solution(mesh):
    tokens = P(("engine", "ep"), None)
    in_specs = (
        tokens,
        tokens,
        tokens,
        P("ep", "engine", None),
        P("ep", "engine", None),
        P("ep", "engine", None),
        P("ep", "engine", None),
        P("ep", None, "engine"),
        P("ep", None, "engine"),
        P("ep", None),
    )
    return jax.shard_map(
        on_device, mesh=mesh, in_specs=in_specs, out_specs=tokens, check_vma=False
    )
```
